128 devices in a mesh: frames: 8 (over y_hi, x), rows: 16 (over y_lo, z, core).
Axes of the slice: x: 4, y: 4 (y_hi: 2, y_lo: 2; y = y_hi * 2 + y_lo), z: 4, core: 2. Of those that a mesh axis runs over, the one named last changes fastest.
Arguments:
- video: bfloat16 [32, 32, 32, 192], P('frames', 'rows'), may hold values from -6 to 6
- w_conv_in: bfloat16 [3, 3, 3, 192, 384], replicated, may hold values from -0.078125 to 0.078125
- w_conv_out: bfloat16 [3, 3, 3, 384, 384], replicated, may hold values from -0.0625 to 0.0625
- w_shortcut: bfloat16 [192, 384], replicated, may hold values from -0.4375 to 0.4375
- w_embed: bfloat16 [1536, 5120], P(None, 'rows'), may hold values from -0.15625 to 0.15625
- w_qkv: bfloat16 [5120, 15360], P(None, 'rows'), may hold values from -0.078125 to 0.078125
Outputs:
- projected: bfloat16 [32, 16, 16, 15360], P('frames', None, None, 'rows')
The draws below stay inside these ranges and needn't reach their ends.
All inputs are finite; a program needn't handle non-finite values.
Results may differ from the reference program's by a relative error of at most 0.009.
Values may be sent and summed in bfloat16 or wider, within the bound.
No kernel may reach another device: no remote copies, remote signals or barrier semaphores. Data moves between devices by JAX's collectives and lax.ppermute only.
A program may use at most 384 MiB of HBM per device.

```python
import jax
import jax.numpy as jnp
from jax import lax

CIN = 192
COUT = 384
D = 5120
W = 32
FRAMES = 32
H = 32


def levels(stream_key, dims, cuts, least, high):
    level = 1.0
    for position, parts in cuts:
        steps = jax.random.uniform(jax.random.fold_in(jax.random.fold_in(stream_key, 6), position), (parts,), jnp.float32, least / len(cuts), high / len(cuts))
        level = level * jnp.repeat(jnp.exp(steps), dims[position] // parts).reshape((-1,) + (1,) * (len(dims) - 1 - position))
    return level


def scatter_about(stream_key, extent, spread, limit, split=(), kind=jnp.bfloat16):
    array = spread * jax.random.normal(stream_key, extent, jnp.float32)
    if split:
        array = array * levels(stream_key, extent, split, -0.22, 0.18)
    return jnp.clip(array, -limit, limit).astype(kind)


def setup_inputs(seed: int = 0) -> dict:
    keys = jax.random.split(jax.random.key(seed), 7)
    return {
        "video": scatter_about(keys[0], (FRAMES, H, W, CIN), 1.0, 6.0, ((0, 8), (1, 16))),
        "w_conv_in": scatter_about(keys[1], (3, 3, 3, CIN, COUT), (27 * CIN) ** -0.5, 0.078125),
        "w_conv_out": scatter_about(keys[2], (3, 3, 3, COUT, COUT), (27 * COUT) ** -0.5, 0.0625),
        "w_shortcut": scatter_about(keys[3], (CIN, COUT), CIN ** -0.5, 0.4375),
        "w_embed": scatter_about(keys[4], (4 * COUT, D), (4 * COUT) ** -0.5, 0.15625, ((1, 16),)),
        "w_qkv": scatter_about(keys[5], (D, 3 * D), D ** -0.5, 0.078125, ((1, 16),)),
    }


def activate(values):
    widened = values.astype(jnp.float32)
    scaled = widened * lax.rsqrt(lax.optimization_barrier(jnp.mean(widened * widened, axis=-1, keepdims=True)) + 1e-06)
    return jax.nn.silu(scaled).astype(jnp.bfloat16)

def convolve(source, kernel):
    frame_total, row_total, col_total = (source.shape[0], source.shape[1], source.shape[2])
    padded = jnp.pad(source, ((2, 0), (1, 1), (1, 1), (0, 0))).astype(jnp.float32)
    summed = jnp.zeros((frame_total, row_total, col_total, kernel.shape[-1]), jnp.float32)
    for frame_lag in range(3):
        for row_lag in range(3):
            for col_lag in range(3):
                window = padded[frame_lag:frame_lag + frame_total, row_lag:row_lag + row_total, col_lag:col_lag + col_total]
                summed = summed + jnp.einsum('fhwc,cd->fhwd', window, kernel[frame_lag, row_lag, col_lag].astype(jnp.float32))
    return summed

def reference(video, w_conv_in, w_conv_out, w_shortcut, w_embed, w_qkv):
    first = activate(video)
    second = activate(convolve(first, w_conv_in))
    shortcut = jnp.einsum('fhwc,cd->fhwd', video.astype(jnp.float32), w_shortcut.astype(jnp.float32))
    sectioned = (convolve(second, w_conv_out) + shortcut).astype(jnp.bfloat16)
    frame_total, row_total, col_total, channels = sectioned.shape
    patches = sectioned.reshape(frame_total, row_total // 2, 2, col_total // 2, 2, channels)
    patches = patches.transpose(0, 1, 3, 2, 4, 5).reshape(frame_total, row_total // 2 * (col_total // 2), 4 * channels)

    def project(tokens):
        embedded = jnp.dot(tokens, w_embed, preferred_element_type=jnp.float32).astype(jnp.bfloat16)
        widened = embedded.astype(jnp.float32)
        centred = widened - lax.optimization_barrier(jnp.mean(widened, axis=-1, keepdims=True))
        normed = (centred * lax.rsqrt(lax.optimization_barrier(jnp.mean(centred * centred, axis=-1, keepdims=True)) + 1e-06)).astype(jnp.bfloat16)
        return jnp.dot(normed, w_qkv, preferred_element_type=jnp.float32).astype(jnp.bfloat16)
    projected = lax.map(project, patches)
    return projected.reshape(frame_total, row_total // 2, col_total // 2, w_qkv.shape[1])
```

```python
import jax
import jax.numpy as jnp
from jax import lax
from jax.experimental import pallas as pl
from jax.experimental.pallas import tpu as pltpu
from jax.sharding import PartitionSpec as P

F32 = jnp.float32
BF16 = jnp.bfloat16
MIB = 1 << 20

FRAMES_PAIRS = 8
ROWS_PAIRS = 16


def along_x(by):
    return [(i, i // 4 * 4 + (i + by) % 4) for i in range(FRAMES_PAIRS)]


SWAP_Y_HI = [(i, i ^ 4) for i in range(FRAMES_PAIRS)]
NEXT_FRAMES = [(i, (i + 1) % FRAMES_PAIRS) for i in range(FRAMES_PAIRS)]


def along_z(by):
    return [(i, i // 8 * 8 + (i + 2 * by) % 8) for i in range(ROWS_PAIRS)]


SWAP_Y_LO = [(i, i ^ 8) for i in range(ROWS_PAIRS)]
SWAP_CORE = [(i, i ^ 1) for i in range(ROWS_PAIRS)]
SWAP_CHIP = [(i, (i + 1) % ROWS_PAIRS if i % 2 else (i - 1) % ROWS_PAIRS) for i in range(ROWS_PAIRS)]


def by_rows(x, pairs):
    return lax.ppermute(x, "rows", pairs)


def by_frames(x, pairs):
    return lax.ppermute(x, "frames", pairs)


def whole(memory=pltpu.VMEM):
    return pl.BlockSpec(memory_space=memory)


def normalized_silu(v):
    u = v * lax.rsqrt(jnp.mean(v * v, axis=-1, keepdims=True) + 1e-06)
    return u / (1.0 + jnp.exp(-u))


def three_columns(v):
    col = lax.broadcasted_iota(jnp.int32, v.shape, 0) % 32
    n = v.shape[0]
    before = jnp.where(col == 0, 0.0, pltpu.roll(v, 1, 0))
    after = jnp.where(col == 31, 0.0, pltpu.roll(v, n - 1, 0))
    return [before.astype(BF16), v.astype(BF16), after.astype(BF16)]


def conv_kernel(
    place, own, side_core, side_chip, back, back_core, back_chip, w_in, w_out, w_short, out, first, second, vin, vout, flat, sems
):
    core, at_first_frames, at_first_rows, at_last_rows = (place[0], place[1], place[2], place[3])
    for k in range(9):
        pltpu.make_async_copy(w_in.at[k], vin.at[k], sems.at[k]).start()
    for k in range(9):
        pltpu.make_async_copy(w_out.at[k], vout.at[k], sems.at[9 + k]).start()

    core_row = jnp.where(core == 0, 4, 0)
    chip_row = 4 - core_row
    for frame, blocks in ((0, (back, back_core, back_chip)), (4, (own, side_core, side_chip))):
        for ref, row in zip(blocks, (2, core_row, chip_row)):
            v = normalized_silu(ref[...].astype(F32).reshape(256, 192))
            if frame == 0:
                v = jnp.where(at_first_frames == 1, 0.0, v)
            if ref is not back and ref is not own:
                outside = jnp.where(row == 0, at_first_rows, at_last_rows)
                v = jnp.where(outside == 1, 0.0, v)
            cols = jnp.concatenate(three_columns(v), axis=1)
            first[pl.ds(frame, 4), pl.ds(row, 2)] = cols.reshape(4, 2, 32, 576)

    acc = None
    for t in range(3):
        for i in range(3):
            k = 3 * t + i
            pltpu.make_async_copy(w_in.at[k], vin.at[k], sems.at[k]).wait()
            term = jnp.dot(first[t : t + 6, i : i + 4].reshape(768, 576), vin[k], preferred_element_type=F32)
            acc = term if acc is None else acc + term
    acc = normalized_silu(acc)
    line = lax.broadcasted_iota(jnp.int32, acc.shape, 0) // 32
    row, frame = line % 4, line // 4
    outside = (
        ((at_first_frames == 1) & (frame < 2))
        | ((at_first_rows == 1) & (row == 0))
        | ((at_last_rows == 1) & (row == 3))
    )
    acc = jnp.where(outside, 0.0, acc)
    for j, cols in enumerate(three_columns(acc)):
        second[:, :, :, 384 * j : 384 * (j + 1)] = cols.reshape(6, 4, 32, 384)

    acc = jnp.dot(own[...].reshape(256, 192), w_short[...], preferred_element_type=F32)
    for t in range(3):
        for i in range(3):
            k = 3 * t + i
            pltpu.make_async_copy(w_out.at[k], vout.at[k], sems.at[9 + k]).wait()
            acc += jnp.dot(second[t : t + 4, i : i + 2].reshape(256, 1152), vout[k], preferred_element_type=F32)
    for n in range(3):
        flat[n] = acc[:, 128 * n : 128 * (n + 1)].reshape(8, 32, 128)
    for f in range(4):
        for a in range(2):
            for b in range(2):
                for n in range(3):
                    part = 384 * (2 * a + b) + 128 * n
                    cols = flat[n, 2 * f + a, pl.ds(b, 16, stride=2), :]
                    out[16 * f : 16 * (f + 1), part : part + 128] = cols.astype(BF16)


def convolutions(place, blocks, w_in, w_out, w_short):
    return pl.pallas_call(
        conv_kernel,
        out_shape=jax.ShapeDtypeStruct((64, 1536), BF16),
        in_specs=[whole(pltpu.SMEM)] + [whole()] * 6 + [whole(pl.ANY)] * 2 + [whole()],
        out_specs=whole(),
        scratch_shapes=[
            pltpu.VMEM((8, 6, 32, 576), BF16),
            pltpu.VMEM((6, 4, 32, 1152), BF16),
            pltpu.VMEM((9, 576, 384), BF16),
            pltpu.VMEM((9, 1152, 384), BF16),
            pltpu.VMEM((3, 8, 32, 128), F32),
            pltpu.SemaphoreType.DMA((18,)),
        ],
        compiler_params=pltpu.CompilerParams(vmem_limit_bytes=40 * MIB),
        cost_estimate=pl.CostEstimate(flops=5 * 10**9, bytes_accessed=13 * 10**6, transcendentals=10**6),
        name="convolutions",
    )(place, *blocks, w_in.reshape(9, 576, 384), w_out.reshape(9, 1152, 384), w_short)


def fold_kernel(chips, core, same, other, w_qkv, out, acc, sums):
    step = pl.program_id(0)
    ones = jnp.ones((16, 320), BF16)
    total, row = None, None
    for ref, place in ((same, core[0]), (other, 1 - core[0])):
        block = ref[0]
        rows = pl.ds(pl.multiple_of(place * 320, 320), 320)
        term = jnp.dot(jnp.concatenate([block, ones], axis=0), w_qkv[rows, :], preferred_element_type=F32)
        part = jnp.sum(block.astype(F32), axis=1, keepdims=True)
        total = term if total is None else total + term
        row = part if row is None else row + part
    row = jnp.broadcast_to(row, (192, 128))

    @pl.when(step == 0)
    def _():
        acc[...] = total
        sums[...] = row

    @pl.when(step > 0)
    def _():
        acc[...] += total
        sums[...] += row

    @pl.when(step == pl.num_programs(0) - 1)
    def _():
        mean = sums[:, :1] * (1.0 / 5120)
        out[...] = (acc[:192] - mean * acc[192:193]).astype(BF16)


def fold(chips, core, same, other, w_qkv):
    grid = pltpu.PrefetchScalarGridSpec(
        num_scalar_prefetch=2,
        grid=(8,),
        in_specs=[
            pl.BlockSpec((1, 192, 320), lambda s, chips, core: (s, 0, 0)),
            pl.BlockSpec((1, 192, 320), lambda s, chips, core: (s, 0, 0)),
            pl.BlockSpec((640, 960), lambda s, chips, core: (chips[s], 0)),
        ],
        out_specs=pl.BlockSpec((192, 960), lambda s, chips, core: (0, 0)),
        scratch_shapes=[pltpu.VMEM((208, 960), F32), pltpu.VMEM((192, 128), F32)],
    )
    return pl.pallas_call(
        fold_kernel,
        out_shape=jax.ShapeDtypeStruct((192, 960), BF16),
        grid_spec=grid,
        compiler_params=pltpu.CompilerParams(vmem_limit_bytes=32 * MIB),
        cost_estimate=pl.CostEstimate(flops=3 * 10**9, bytes_accessed=12 * 10**6, transcendentals=0),
        name="fold",
    )(chips, core, same, other, w_qkv)


def place_blocks(rows_at, pieces, target, sems):
    copies, block = [], 0
    for n, piece in enumerate(pieces):
        for k in range(piece.shape[0] // 64):
            copies.append(
                pltpu.make_async_copy(piece.at[pl.ds(64 * k, 64)], target.at[rows_at[block]], sems.at[block])
            )
            block += 1
    return copies


def moments_kernel(count, rows_at, *refs):
    pieces, w_embed, out, tokens, sems = (refs[:count], refs[count], refs[count + 1], refs[count + 2], refs[count + 3])
    copies = place_blocks(rows_at, pieces, tokens, sems)
    for copy in copies:
        copy.start()
    for copy in copies:
        copy.wait()
    lane = lax.broadcasted_iota(jnp.int32, (256, 128), 1)
    for g in range(4):
        e = jnp.dot(tokens[4 * g : 4 * g + 4].reshape(256, 1536), w_embed[...], preferred_element_type=F32)
        mean = jnp.mean(e, axis=1, keepdims=True)
        spread = jnp.sum((e - mean) * (e - mean), axis=1, keepdims=True)
        turned = jnp.where(lane == 0, mean, spread).T
        out[g : g + 1, :] = turned[0:1, :]
        out[4 + g : 5 + g, :] = turned[1:2, :]


def moments(rows_at, pieces, w_embed):
    count = len(pieces)
    return pl.pallas_call(
        lambda *refs: moments_kernel(count, *refs),
        out_shape=jax.ShapeDtypeStruct((8, 256), F32),
        in_specs=[whole(pltpu.SMEM)] + [whole(pl.ANY)] * count + [whole()],
        out_specs=whole(),
        scratch_shapes=[pltpu.VMEM((16, 64, 1536), BF16), pltpu.SemaphoreType.DMA((16,))],
        compiler_params=pltpu.CompilerParams(vmem_limit_bytes=32 * MIB),
        cost_estimate=pl.CostEstimate(flops=10**9, bytes_accessed=5 * 10**6, transcendentals=0),
        name="moments",
    )(rows_at, *pieces, w_embed)


def merged(parts, features):
    mean = sum(part[:4] for part in parts) * (1.0 / len(parts))
    spread = sum(part[4:] for part in parts)
    spread = spread + features * sum((part[:4] - mean) * (part[:4] - mean) for part in parts)
    return jnp.concatenate([mean, spread], axis=0)


def project_kernel(count, layout, rows_at, fold_at, *refs):
    pieces, refs = refs[:count], refs[count:]
    weights, refs = refs[: len(layout)], refs[len(layout) :]
    stats, out, tokens, folded, sems, fold_sems = refs
    copies = place_blocks(rows_at, pieces, tokens, sems)
    for n, (ref, (source, size, at, inside)) in enumerate(zip(weights, layout)):
        start = pl.multiple_of(fold_at[at] * 192 + inside, 96)
        copies.append(
            pltpu.make_async_copy(ref.at[pl.ds(source, size)], folded.at[pl.ds(start, size)], fold_sems.at[n])
        )
    for copy in copies:
        copy.start()
    for copy in copies:
        copy.wait()
    for g in range(4):
        acc = jnp.dot(tokens[4 * g : 4 * g + 4].reshape(256, 1536), folded[...], preferred_element_type=F32)
        scale = lax.rsqrt(stats[4 + g : 5 + g, :] * (1.0 / 5120) + 1e-06)
        scale = jnp.broadcast_to(scale, (128, 256)).T[:, :1]
        result = (acc * scale).astype(BF16).reshape(4, 4, 16, 960)
        for r in range(4):
            out[:, 4 * g + r] = result[r]


def project(rows_at, fold_at, pieces, weights, layout, stats):
    count = len(pieces)
    return pl.pallas_call(
        lambda *refs: project_kernel(count, layout, *refs),
        out_shape=jax.ShapeDtypeStruct((4, 16, 16, 960), BF16),
        in_specs=[whole(pltpu.SMEM)] * 2 + [whole(pl.ANY)] * (count + len(weights)) + [whole()],
        out_specs=whole(),
        scratch_shapes=[
            pltpu.VMEM((16, 64, 1536), BF16),
            pltpu.VMEM((1536, 960), BF16),
            pltpu.SemaphoreType.DMA((16,)),
            pltpu.SemaphoreType.DMA((len(weights),)),
        ],
        compiler_params=pltpu.CompilerParams(vmem_limit_bytes=40 * MIB),
        cost_estimate=pl.CostEstimate(flops=3 * 10**9, bytes_accessed=8 * 10**6, transcendentals=0),
        name="project",
    )(rows_at, fold_at, *pieces, *weights, stats)


def shards(video, w_conv_in, w_conv_out, w_shortcut, w_embed, w_qkv):
    f, r = lax.axis_index("frames"), lax.axis_index("rows")
    y_hi, x = f // 4, f % 4
    y_lo, z, core = r // 8, r // 2 % 4, r % 2

    mine = lax.dynamic_slice_in_dim(w_embed, f * 192, 192, axis=0)
    near = jnp.stack([mine, by_rows(mine, SWAP_Y_LO)])
    same = jnp.concatenate([near] + [by_rows(near, along_z(by)) for by in (1, -1, 2)])
    other = by_rows(same, SWAP_CORE)
    chips = jnp.stack([(y_lo ^ b) * 4 + (z - by) % 4 for by in (0, 1, -1, 2) for b in (0, 1)]).astype(jnp.int32)
    folded = fold(chips, core.astype(jnp.int32).reshape(1), same, other, w_qkv)

    from_left, from_right = by_frames(folded, along_x(1)), by_frames(folded, along_x(-1))
    across = by_frames(folded, SWAP_Y_HI)
    far_left = by_frames(jnp.concatenate([from_left[:96], across]), along_x(1))
    far_right = by_frames(jnp.concatenate([from_right[96:], across]), along_x(-1))
    last_left = by_frames(far_left[96:192], along_x(1))
    last_right = by_frames(far_right[192:], along_x(-1))
    weights = [folded, from_left, from_right, across, far_left, far_left, far_right, far_right, last_left, last_right]
    layout = [
        (0, 192, 0, 0),
        (0, 192, 1, 0),
        (0, 192, 2, 0),
        (0, 192, 4, 0),
        (0, 96, 3, 0),
        (96, 192, 5, 0),
        (0, 96, 3, 96),
        (96, 192, 6, 0),
        (0, 96, 7, 0),
        (0, 96, 7, 96),
    ]
    fold_at = jnp.stack([(y_hi ^ h) * 4 + (x + by) % 4 for h in (0, 1) for by in (0, -1, 1, 2)]).astype(jnp.int32)

    back = by_frames(video, NEXT_FRAMES)
    side_core, side_chip = by_rows(video, SWAP_CORE), by_rows(video, SWAP_CHIP)
    back_core, back_chip = by_rows(back, SWAP_CORE), by_rows(back, SWAP_CHIP)
    place = jnp.stack([core, f == 0, r == 0, r == 15]).astype(jnp.int32)
    patches = convolutions(
        place, (video, side_core, side_chip, back, back_core, back_chip), w_conv_in, w_conv_out, w_shortcut
    )

    near = jnp.concatenate([patches, by_rows(patches, SWAP_Y_LO)])
    from_low, from_high = by_rows(near, along_z(1)), by_rows(near, along_z(-1))
    far_low = by_rows(from_low[:64], along_z(1))
    far_high = by_rows(from_high[64:], along_z(-1))
    most = jnp.concatenate([near, from_low, from_high])
    rest = jnp.concatenate([far_low, far_high])
    pieces = [most, rest, by_rows(most, SWAP_CORE), by_rows(rest, SWAP_CORE)]
    rows_at = jnp.stack(
        [
            ((y_lo ^ b) * 4 + (z + by) % 4) * 2 + (core ^ c)
            for c in (0, 1)
            for by in (0, -1, 1, 2)
            for b in (0, 1)
        ]
    ).astype(jnp.int32)

    stats = moments(rows_at, pieces, w_embed)
    stats = merged([stats, by_rows(stats, SWAP_Y_LO)], 320)
    stats = merged([stats] + [by_rows(stats, along_z(by)) for by in (1, -1, 2)], 640)
    stats = merged([stats, by_rows(stats, SWAP_CORE)], 2560)
    return project(rows_at, fold_at, pieces, weights, layout, stats)


def solution(mesh):
    placed = (P("frames", "rows", None, None), P(), P(), P(), P(None, "rows"), P(None, "rows"))
    return jax.shard_map(
        shards,
        mesh=mesh,
        in_specs=placed,
        out_specs=P("frames", None, None, "rows"),
        check_vma=False,
    )
```

```python
import jax
import jax.numpy as jnp
from jax import lax
from jax.experimental import pallas as pl
from jax.experimental.pallas import tpu as pltpu
from jax.sharding import PartitionSpec as P

F32 = jnp.float32
BF16 = jnp.bfloat16
MIB = 1 << 20

FRAMES_PAIRS = 8
ROWS_PAIRS = 16


def along_x(by):
    return [(i, i // 4 * 4 + (i + by) % 4) for i in range(FRAMES_PAIRS)]


SWAP_Y_HI = [(i, i ^ 4) for i in range(FRAMES_PAIRS)]
NEXT_FRAMES = [(i, (i + 1) % FRAMES_PAIRS) for i in range(FRAMES_PAIRS)]


def along_z(by):
    return [(i, i // 8 * 8 + (i + 2 * by) % 8) for i in range(ROWS_PAIRS)]


SWAP_Z, SWAP_Z_RING = ([(i, i ^ 2) for i in range(ROWS_PAIRS)], [(i, i ^ 6) for i in range(ROWS_PAIRS)])


SWAP_Y_LO = [(i, i ^ 8) for i in range(ROWS_PAIRS)]
SWAP_CORE = [(i, i ^ 1) for i in range(ROWS_PAIRS)]
SWAP_CHIP = [(i, (i + 1) % ROWS_PAIRS if i % 2 else (i - 1) % ROWS_PAIRS) for i in range(ROWS_PAIRS)]
NEXT_FRAMES_SWAP_CHIP = [(a * ROWS_PAIRS + c, b * ROWS_PAIRS + d) for a, b in NEXT_FRAMES for c, d in SWAP_CHIP]


def by_rows(x, pairs):
    return lax.ppermute(x, "rows", pairs)


def by_frames(x, pairs):
    return lax.ppermute(x, "frames", pairs)


def here():
    return lax.axis_index("frames"), lax.axis_index("rows")


def at_chip(place, y_lo, z):
    rows = place[1]
    return (rows // 8 + y_lo) % 2 * 4 + (rows // 2 + z) % 4


def at_rows(place, y_lo, z, core):
    return at_chip(place, y_lo, z) * 2 + (place[1] + core) % 2


def at_frames(place, y_hi, x):
    return (place[0] // 4 + y_hi) % 2 * 4 + (place[0] + x) % 4


def whole(memory=pltpu.VMEM):
    return pl.BlockSpec(memory_space=memory)


def in_hbm(*arrays):
    return [pltpu.with_memory_space_constraint(array, pltpu.HBM) for array in arrays]


def in_vmem(*arrays):
    return [pltpu.with_memory_space_constraint(array, pltpu.VMEM) for array in arrays]


def normalized_silu(v):
    u = v * lax.rsqrt(jnp.mean(v * v, axis=-1, keepdims=True) + 1e-06)
    half = 0.5 * u
    return half + half * jnp.tanh(half)


def over_columns(v):
    n, c = v.shape[0], v.shape[1] // 3
    col = lax.broadcasted_iota(jnp.int32, (n, c), 0) & 31
    before = jnp.where(col == 0, 0.0, pltpu.roll(v[:, :c], 1, 0))
    after = jnp.where(col == 31, 0.0, pltpu.roll(v[:, 2 * c :], n - 1, 0))
    return v[:, c : 2 * c] + before + after


def taps(ref, frames, rows):
    n, c = frames * rows * 32, ref.shape[-1]
    windows = [ref[t : t + frames, i : i + rows].reshape(n, c) for t in range(3) for i in range(3)]
    return jnp.concatenate(windows, axis=1)


def conv_kernel(
    side_core, side_chip, back, back_core, back_chip, video, w_in, w_out, shortcut,
    out, first, second, vin, vout, flat, own, w_short, sems,
):
    place = here()
    core = place[1] % 2
    at_first_frames, at_first_rows, at_last_rows = (place[0] == 0, place[1] == 0, place[1] == 15)
    small = [pltpu.make_async_copy(video, own, sems.at[54]), pltpu.make_async_copy(shortcut, w_short, sems.at[55])]
    for load in small:
        load.start()
    loads = []
    for n, (source, target, size) in enumerate(((w_in, vin, 192), (w_out, vout, 384))):
        loads.append(
            [
                pltpu.make_async_copy(
                    source.at[3 * k + j],
                    target.at[pl.ds(size * k, size), pl.ds(384 * j, 384)],
                    sems.at[27 * n + 3 * k + j],
                )
                for k in range(9)
                for j in range(3)
            ]
        )
    for load in loads[0]:
        load.start()

    core_row = jnp.where(core == 0, 4, 0)
    chip_row = 4 - core_row
    for frame, blocks in ((0, (back, back_core, back_chip)), (4, (own, side_core, side_chip))):
        for ref, row in zip(blocks, (2, core_row, chip_row)):
            if ref is own:
                small[0].wait()
            v = normalized_silu(ref[...].astype(F32).reshape(256, 192))
            first[pl.ds(frame, 4), pl.ds(row, 2)] = v.astype(BF16).reshape(4, 2, 32, 192)

    @pl.when(at_first_frames)
    def _():
        first[0:4] = jnp.zeros((4, 6, 32, 192), BF16)

    @pl.when(at_first_rows)
    def _():
        first[:, 0:2] = jnp.zeros((8, 2, 32, 192), BF16)

    @pl.when(at_last_rows)
    def _():
        first[:, 4:6] = jnp.zeros((8, 2, 32, 192), BF16)

    for load in loads[0]:
        load.wait()
    for load in loads[1]:
        load.start()
    acc = over_columns(jnp.dot(taps(first, 6, 4), vin[...], preferred_element_type=F32))
    second[...] = normalized_silu(acc).astype(BF16).reshape(6, 4, 32, 384)

    @pl.when(at_first_frames)
    def _():
        second[0:2] = jnp.zeros((2, 4, 32, 384), BF16)

    @pl.when(at_first_rows)
    def _():
        second[:, 0:1] = jnp.zeros((6, 1, 32, 384), BF16)

    @pl.when(at_last_rows)
    def _():
        second[:, 3:4] = jnp.zeros((6, 1, 32, 384), BF16)

    for load in loads[1]:
        load.wait()
    acc = over_columns(jnp.dot(taps(second, 4, 2), vout[...], preferred_element_type=F32))
    small[1].wait()
    acc = acc + jnp.dot(own[...].reshape(256, 192), w_short[...], preferred_element_type=F32)
    for n in range(3):
        flat[n] = acc[:, 128 * n : 128 * (n + 1)].reshape(8, 32, 128)
    for f in range(4):
        for a in range(2):
            for b in range(2):
                for n in range(3):
                    part = 384 * (2 * a + b) + 128 * n
                    cols = flat[n, 2 * f + a, pl.ds(b, 16, stride=2), :]
                    out[16 * f : 16 * (f + 1), part : part + 128] = cols.astype(BF16)


def convolutions(video, blocks, w_in, w_out, w_short):
    return pl.pallas_call(
        conv_kernel,
        out_shape=pltpu.VMEM((64, 1536), BF16),
        in_specs=[whole()] * 5 + [whole(pltpu.HBM)] * 4,
        out_specs=whole(),
        scratch_shapes=[
            pltpu.VMEM((8, 6, 32, 192), BF16),
            pltpu.VMEM((6, 4, 32, 384), BF16),
            pltpu.VMEM((1728, 1152), BF16),
            pltpu.VMEM((3456, 1152), BF16),
            pltpu.VMEM((3, 8, 32, 128), F32),
            pltpu.VMEM((4, 2, 32, 192), BF16),
            pltpu.VMEM((192, 384), BF16),
            pltpu.SemaphoreType.DMA((56,)),
        ],
        compiler_params=pltpu.CompilerParams(vmem_limit_bytes=40 * MIB),
        cost_estimate=pl.CostEstimate(flops=8 * 10**9, bytes_accessed=13 * 10**6, transcendentals=10**6),
        name="convolutions",
    )(*in_vmem(*blocks), *in_hbm(video, w_in.reshape(27, 192, 384), w_out.reshape(27, 384, 384), w_short))


def fold_kernel(*refs):
    place = here()
    count = (len(refs) - 3) // 2
    w_qkv, out, rows = refs[2 * count :]
    core = place[1] % 2
    rows[:, 128:] = jnp.ones((5120, 128), BF16)
    chips = []
    for same, other in zip(refs[:count], refs[count : 2 * count]):
        for n in range(same.shape[0] // 480):
            s = len(chips)
            chips.append(at_chip(place, s // 4, (0, -1, 1, 2)[s % 4]))
            for ref, at in ((same, core), (other, 1 - core)):
                block = ref[480 * n : 480 * (n + 1)]
                first = pl.multiple_of(640 * s + 320 * at, 32)
                rows[pl.ds(first, 320), :128] = block[:320]
                rows[pl.ds(first, 160), 128:192] = block[320:, :64]
                rows[pl.ds(first + 160, 160), 128:192] = block[320:, 64:]
    total, mean = None, None
    for s, chip in enumerate(chips):
        slab, part = w_qkv[:, pl.ds(pl.multiple_of(chip * 640, 128), 640)], rows[640 * s : 640 * (s + 1)]
        term = jnp.dot(slab, part, preferred_element_type=F32)
        part = jnp.sum(part.astype(F32), axis=0, keepdims=True)
        total = term if total is None else total + term
        mean = part if mean is None else mean + part
    total = total - total[:, 192:193] * (mean * (1.0 / 5120))
    turned = jnp.concatenate([total, jnp.zeros((64, 256), F32)], axis=0).T
    out[...] = turned[:192, :960].astype(BF16)


def fold(same, other, w_qkv):
    return pl.pallas_call(
        fold_kernel,
        out_shape=pltpu.VMEM((192, 960), BF16),
        in_specs=[whole()] * (2 * len(same) + 1),
        out_specs=whole(),
        scratch_shapes=[pltpu.VMEM((5120, 256), BF16)],
        compiler_params=pltpu.CompilerParams(vmem_limit_bytes=20 * MIB),
        cost_estimate=pl.CostEstimate(flops=4 * 10**9, bytes_accessed=12 * 10**6, transcendentals=0),
        name="fold",
    )(*in_vmem(*same, *other, w_qkv.T))


def moments_kernel(layout, *refs):
    place = here()
    count = len(layout)
    pieces, w_embed, out, tokens = (refs[:count], refs[count], refs[count + 1], refs[count + 2])
    for ref, parts in zip(pieces, layout):
        for source, size, block, at in parts:
            tokens[at_rows(place, *block), at : at + size] = ref[source : source + size]
    for g in range(4):
        e = lax.dot_general(
            w_embed[...],
            tokens[4 * g : 4 * g + 4].reshape(256, 1536),
            (((1,), (1,)), ((), ())),
            preferred_element_type=F32,
        )
        mean = jnp.mean(e, axis=0, keepdims=True)
        out[g : g + 1, :] = mean
        out[4 + g : 5 + g, :] = jnp.sum((e - mean) * (e - mean), axis=0, keepdims=True)


def moments(pieces, layout, w_embed):
    return pl.pallas_call(
        lambda *refs: moments_kernel(layout, *refs),
        out_shape=[pltpu.VMEM((8, 256), F32), pltpu.VMEM((16, 64, 1536), BF16)],
        in_specs=[whole()] * (len(pieces) + 1),
        out_specs=[whole(), whole()],
        compiler_params=pltpu.CompilerParams(vmem_limit_bytes=20 * MIB),
        cost_estimate=pl.CostEstimate(flops=2 * 10**9, bytes_accessed=5 * 10**6, transcendentals=0),
        name="moments",
    )(*in_vmem(*pieces), w_embed.T)


def merge_kernel(features, *refs):
    parts, out = [ref[...] for ref in refs[:-1]], refs[-1]
    mean = sum(part[:4] for part in parts) * (1.0 / len(parts))
    spread = sum(part[4:] for part in parts)
    spread = spread + features * sum((part[:4] - mean) * (part[:4] - mean) for part in parts)
    out[:4] = mean
    out[4:] = spread


def merged(parts, features):
    return pl.pallas_call(
        lambda *refs: merge_kernel(features, *refs),
        out_shape=pltpu.VMEM((8, 256), F32),
        in_specs=[whole()] * len(parts),
        out_specs=whole(),
        compiler_params=pltpu.CompilerParams(vmem_limit_bytes=2 * MIB),
        cost_estimate=pl.CostEstimate(flops=10**6, bytes_accessed=10**5, transcendentals=0),
        name="merge",
    )(*in_vmem(*parts))


def most_kernel(layout, tokens, *refs):
    place = here()
    count = len(layout)
    weights, out, folded = (refs[:count], refs[count], refs[count + 1])
    for ref, parts in zip(weights, layout):
        for source, size, block, at in parts:
            folded[pl.ds(pl.multiple_of(at_frames(place, *block) * 192 + at, 96), size), :] = ref[source : source + size]
    folded[pl.ds(pl.multiple_of(at_frames(place, 1, 2) * 192, 192), 192), :] = jnp.zeros((192, 960), BF16)
    for g in range(4):
        x = tokens[4 * g : 4 * g + 4].reshape(256, 1536)
        out[256 * g : 256 * (g + 1)] = jnp.dot(x, folded[...], preferred_element_type=F32)


def project_most(tokens, weights, layout):
    return pl.pallas_call(
        lambda *refs: most_kernel(layout, *refs),
        out_shape=pltpu.VMEM((1024, 960), F32),
        in_specs=[whole()] * (len(weights) + 1),
        out_specs=whole(),
        scratch_shapes=[pltpu.VMEM((1536, 960), BF16)],
        compiler_params=pltpu.CompilerParams(vmem_limit_bytes=20 * MIB),
        cost_estimate=pl.CostEstimate(flops=4 * 10**9, bytes_accessed=8 * 10**6, transcendentals=0),
        name="project_most",
    )(*in_vmem(tokens, *weights))


def last_kernel(tokens, total, low, high, stats, out, folded, staged, sems):
    place = here()
    last = at_frames(place, 1, 2)
    pair, half = last // 2, last % 2
    folded[...] = jnp.zeros((384, 960), BF16)
    folded[pl.ds(pl.multiple_of(half * 192, 192), 96), :] = low[...]
    folded[pl.ds(pl.multiple_of(half * 192 + 96, 96), 96), :] = high[...]
    copies = []
    for g in range(4):
        x = tokens[4 * g : 4 * g + 4, :, pl.ds(pl.multiple_of(pair * 384, 128), 384)].reshape(256, 384)
        acc = total[256 * g : 256 * (g + 1)] + jnp.dot(x, folded[...], preferred_element_type=F32)
        scale = lax.rsqrt(stats[4 + g : 5 + g, :] * (1.0 / 5120) + 1e-06)
        scale = jnp.broadcast_to(scale, (128, 256)).T[:, :1]
        result = (acc * scale).astype(BF16).reshape(4, 4, 16, 960)
        for r in range(4):
            staged[:, 4 * g + r] = result[r]
        copies.append(
            pltpu.make_async_copy(staged.at[:, pl.ds(4 * g, 4)], out.at[:, pl.ds(4 * g, 4)], sems.at[g])
        )
        copies[g].start()
    for copy in copies:
        copy.wait()


def project_last(tokens, total, low, high, stats):
    return pl.pallas_call(
        last_kernel,
        out_shape=jax.ShapeDtypeStruct((4, 16, 16, 960), BF16),
        in_specs=[whole()] * 5,
        out_specs=whole(pltpu.HBM),
        scratch_shapes=[
            pltpu.VMEM((384, 960), BF16),
            pltpu.VMEM((4, 16, 16, 960), BF16),
            pltpu.SemaphoreType.DMA((4,)),
        ],
        compiler_params=pltpu.CompilerParams(vmem_limit_bytes=32 * MIB),
        cost_estimate=pl.CostEstimate(flops=2 * 10**9, bytes_accessed=8 * 10**6, transcendentals=0),
        name="project_last",
    )(*in_vmem(tokens, total, low, high, stats))


def slice_kernel(w_embed, out, slab, sem):
    place = here()
    load = pltpu.make_async_copy(w_embed.at[:, pl.ds(pl.multiple_of(place[0] // 2 * 384, 128), 384)], slab, sem)
    load.start()
    load.wait()
    mine = jnp.where(place[0] % 2 == 0, slab[:, :192], slab[:, 192:])
    out[:320] = mine[:, :128]
    out[320:] = jnp.concatenate([mine[:160, 128:], mine[160:, 128:]], axis=1)


def spliced(name, *targets):
    arrays = []
    for array in [part[0] for target in targets for part in target]:
        if not any(array is other for other in arrays):
            arrays.append(array)
    places = [[next(n for n, a in enumerate(arrays) if a is part[0]) for part in target] for target in targets]

    def kernel(*refs):
        for out, target, sources in zip(refs[len(arrays) :], targets, places):
            at = 0
            for (_, start, size), n in zip(target, sources):
                out[at : at + size] = refs[n][start : start + size]
                at += size

    rows = [sum(part[2] for part in target) for target in targets]
    columns = targets[0][0][0].shape[1]
    return pl.pallas_call(
        kernel,
        out_shape=[pltpu.VMEM((n, columns), BF16) for n in rows],
        in_specs=[whole()] * len(arrays),
        out_specs=[whole()] * len(targets),
        compiler_params=pltpu.CompilerParams(vmem_limit_bytes=8 * MIB),
        cost_estimate=pl.CostEstimate(flops=10**6, bytes_accessed=10**6, transcendentals=0),
        name=name,
    )(*in_vmem(*arrays))


def embed_slice(w_embed):
    return pl.pallas_call(
        slice_kernel,
        out_shape=pltpu.VMEM((480, 128), BF16),
        in_specs=[whole(pltpu.HBM)],
        out_specs=whole(),
        scratch_shapes=[pltpu.VMEM((320, 384), BF16), pltpu.SemaphoreType.DMA],
        cost_estimate=pl.CostEstimate(flops=10**6, bytes_accessed=10**6, transcendentals=0),
        name="embed_slice",
    )(*in_hbm(w_embed.T))


def shards(video, w_conv_in, w_conv_out, w_shortcut, w_embed, w_qkv):
    back = by_frames(video, NEXT_FRAMES)
    back_chip = lax.ppermute(video, ("frames", "rows"), NEXT_FRAMES_SWAP_CHIP)
    side_core, side_chip = by_rows(video, SWAP_CORE), by_rows(video, SWAP_CHIP)
    mine = embed_slice(w_embed)
    along = [by_rows(mine, along_z(by)) for by in (1, -1, 2)]
    along, back, back_chip, side_chip = lax.optimization_barrier((along, back, back_chip, side_chip))
    back_core = by_rows(back, SWAP_CORE)
    (four,) = spliced("embed_four", [(mine, 0, 480)] + [(part, 0, 480) for part in along])
    patches = convolutions(
        video, (side_core, side_chip, back, back_core, back_chip), w_conv_in, w_conv_out, w_shortcut
    )
    across = by_rows(four, SWAP_Y_LO)
    across, patches = lax.optimization_barrier((across, patches))
    folded = fold([four, across], [by_rows(four, SWAP_CORE), by_rows(across, SWAP_CORE)], w_qkv)

    opposite = by_rows(patches, SWAP_Y_LO)
    opposite, folded = lax.optimization_barrier((opposite, folded))
    (pair,) = spliced("patch_pair", [(patches, 0, 64), (opposite, 0, 64)])
    from_low, from_high = by_rows(pair, along_z(1)), by_rows(pair, along_z(-1))
    up, down = spliced("patch_ends", [(from_low, 0, 64)], [(from_high, 64, 64)])
    last_low, last_high = by_rows(up, along_z(1)), by_rows(down, along_z(-1))
    groups = [pair, from_low, from_high, last_low, last_high]
    pieces = groups + [by_rows(group, SWAP_CORE) for group in groups]
    pieces_layout = [
        layout
        for core in (0, 1)
        for layout in (
            [(0, 64, (0, 0, core), 0), (64, 64, (1, 0, core), 0)],
            [(0, 64, (0, -1, core), 0), (64, 64, (1, -1, core), 0)],
            [(0, 64, (0, 1, core), 0), (64, 64, (1, 1, core), 0)],
            [(0, 64, (0, 2, core), 0)],
            [(0, 64, (1, 2, core), 0)],
        )
    ]

    from_left, from_right = by_frames(folded, along_x(1)), by_frames(folded, along_x(-1))
    across = by_frames(folded, SWAP_Y_HI)
    to_right, to_left = spliced(
        "fold_parts", ((from_left, 0, 96), (across, 0, 192)), ((from_right, 96, 96), (across, 0, 192))
    )
    far_left, far_right = by_frames(to_right, along_x(1)), by_frames(to_left, along_x(-1))
    to_right, to_left = spliced("fold_ends", ((far_left, 96, 96),), ((far_right, 192, 96),))
    last_left, last_right = by_frames(to_right, along_x(1)), by_frames(to_left, along_x(-1))
    weights = [folded, from_left, from_right, across, far_left, far_right]
    weights_layout = [
        [(0, 192, (0, 0), 0)],
        [(0, 192, (0, -1), 0)],
        [(0, 192, (0, 1), 0)],
        [(0, 192, (1, 0), 0)],
        [(0, 96, (0, 2), 0), (96, 192, (1, -1), 0)],
        [(0, 96, (0, 2), 96), (96, 192, (1, 1), 0)],
    ]

    stats, tokens = moments(pieces, pieces_layout, w_embed)
    total = project_most(tokens, weights, weights_layout)
    for pairs, features in ((SWAP_Y_LO, 320), (SWAP_Z, 640), (SWAP_Z_RING, 1280), (SWAP_CORE, 2560)):
        swapped = by_rows(stats, pairs)
        if pairs is SWAP_Z_RING:
            swapped, total = lax.optimization_barrier((swapped, total))
        stats = merged([stats, swapped], features)
    return project_last(tokens, total, last_left, last_right, stats)


def solution(mesh):
    placed = (P("frames", "rows", None, None), P(), P(), P(), P(None, "rows"), P(None, "rows"))
    return jax.shard_map(
        shards,
        mesh=mesh,
        in_specs=placed,
        out_specs=P("frames", None, None, "rows"),
        check_vma=False,
    )
```

```python
import jax
import jax.numpy as jnp
from jax import lax
from jax.experimental import pallas as pl
from jax.experimental.pallas import tpu as pltpu
from jax.sharding import PartitionSpec as P

F32 = jnp.float32
BF16 = jnp.bfloat16
MIB = 1 << 20

FRAMES_PAIRS = 8
ROWS_PAIRS = 16


def swap_x(k):
    return [(i, i ^ k) for i in range(FRAMES_PAIRS)]


def swap_z(k):
    return [(i, i ^ (2 * k)) for i in range(ROWS_PAIRS)]


SWAP_Y_HI = [(i, i ^ 4) for i in range(FRAMES_PAIRS)]
NEXT_FRAMES = [(i, (i + 1) % FRAMES_PAIRS) for i in range(FRAMES_PAIRS)]
SWAP_Y_LO = [(i, i ^ 8) for i in range(ROWS_PAIRS)]
SWAP_CORE = [(i, i ^ 1) for i in range(ROWS_PAIRS)]
SWAP_CHIP = [(i, (i + 1) % ROWS_PAIRS if i % 2 else (i - 1) % ROWS_PAIRS) for i in range(ROWS_PAIRS)]
NEXT_FRAMES_SWAP_CHIP = [(a * ROWS_PAIRS + c, b * ROWS_PAIRS + d) for a, b in NEXT_FRAMES for c, d in SWAP_CHIP]


def by_rows(x, pairs):
    return lax.ppermute(x, "rows", pairs)


def by_frames(x, pairs):
    return lax.ppermute(x, "frames", pairs)


def here():
    return lax.axis_index("frames"), lax.axis_index("rows")


def at_chip(place, y_lo, z):
    rows = place[1]
    return (rows // 8 + y_lo) % 2 * 4 + (rows // 2 % 4 ^ z)


def at_rows(place, y_lo, z, core):
    return at_chip(place, y_lo, z) * 2 + (place[1] + core) % 2


def at_frames(place, y_hi, x):
    return (place[0] // 4 + y_hi) % 2 * 4 + (place[0] % 4 ^ x)


def whole(memory=pltpu.VMEM):
    return pl.BlockSpec(memory_space=memory)


def in_hbm(*arrays):
    return [pltpu.with_memory_space_constraint(array, pltpu.HBM) for array in arrays]


def in_vmem(*arrays):
    return [pltpu.with_memory_space_constraint(array, pltpu.VMEM) for array in arrays]


def normalized_silu(v):
    u = v * lax.rsqrt(jnp.mean(v * v, axis=-1, keepdims=True) + 1e-06)
    half = 0.5 * u
    return half + half * jnp.tanh(half)


def over_columns(v):
    n, c = v.shape[0], v.shape[1] // 3
    col = lax.broadcasted_iota(jnp.int32, (n, c), 0) & 31
    before = jnp.where(col == 0, 0.0, pltpu.roll(v[:, :c], 1, 0))
    after = jnp.where(col == 31, 0.0, pltpu.roll(v[:, 2 * c :], n - 1, 0))
    return v[:, c : 2 * c] + before + after


def taps(ref, frames, rows):
    n, c = frames * rows * 32, ref.shape[-1]
    windows = [ref[t : t + frames, i : i + rows].reshape(n, c) for t in range(3) for i in range(3)]
    return jnp.concatenate(windows, axis=1)


def conv_kernel(
    side_core, side_chip, back, back_core, back_chip, video, w_in, w_out, shortcut,
    out, first, second, vin, vout, flat, own, w_short, sems,
):
    place = here()
    core = place[1] % 2
    at_first_frames, at_first_rows, at_last_rows = (place[0] == 0, place[1] == 0, place[1] == 15)
    small = [pltpu.make_async_copy(video, own, sems.at[54]), pltpu.make_async_copy(shortcut, w_short, sems.at[55])]
    for load in small:
        load.start()
    loads = []
    for n, (source, target, size) in enumerate(((w_in, vin, 192), (w_out, vout, 384))):
        loads.append(
            [
                pltpu.make_async_copy(
                    source.at[3 * k + j],
                    target.at[pl.ds(size * k, size), pl.ds(384 * j, 384)],
                    sems.at[27 * n + 3 * k + j],
                )
                for k in range(9)
                for j in range(3)
            ]
        )
    for load in loads[0]:
        load.start()

    core_row = jnp.where(core == 0, 4, 0)
    chip_row = 4 - core_row
    for frame, blocks in ((0, (back, back_core, back_chip)), (4, (own, side_core, side_chip))):
        for ref, row in zip(blocks, (2, core_row, chip_row)):
            if ref is own:
                small[0].wait()
            v = normalized_silu(ref[...].astype(F32).reshape(256, 192))
            first[pl.ds(frame, 4), pl.ds(row, 2)] = v.astype(BF16).reshape(4, 2, 32, 192)

    @pl.when(at_first_frames)
    def _():
        first[0:4] = jnp.zeros((4, 6, 32, 192), BF16)

    @pl.when(at_first_rows)
    def _():
        first[:, 0:2] = jnp.zeros((8, 2, 32, 192), BF16)

    @pl.when(at_last_rows)
    def _():
        first[:, 4:6] = jnp.zeros((8, 2, 32, 192), BF16)

    for load in loads[0]:
        load.wait()
    for load in loads[1]:
        load.start()
    acc = over_columns(jnp.dot(taps(first, 6, 4), vin[...], preferred_element_type=F32))
    second[...] = normalized_silu(acc).astype(BF16).reshape(6, 4, 32, 384)

    @pl.when(at_first_frames)
    def _():
        second[0:2] = jnp.zeros((2, 4, 32, 384), BF16)

    @pl.when(at_first_rows)
    def _():
        second[:, 0:1] = jnp.zeros((6, 1, 32, 384), BF16)

    @pl.when(at_last_rows)
    def _():
        second[:, 3:4] = jnp.zeros((6, 1, 32, 384), BF16)

    for load in loads[1]:
        load.wait()
    acc = over_columns(jnp.dot(taps(second, 4, 2), vout[...], preferred_element_type=F32))
    small[1].wait()
    acc = acc + jnp.dot(own[...].reshape(256, 192), w_short[...], preferred_element_type=F32)
    for n in range(3):
        flat[n] = acc[:, 128 * n : 128 * (n + 1)].reshape(8, 32, 128)
    for f in range(4):
        for a in range(2):
            for b in range(2):
                for n in range(3):
                    part = 384 * (2 * a + b) + 128 * n
                    cols = flat[n, 2 * f + a, pl.ds(b, 16, stride=2), :]
                    out[16 * f : 16 * (f + 1), part : part + 128] = cols.astype(BF16)


def convolutions(video, blocks, w_in, w_out, w_short):
    return pl.pallas_call(
        conv_kernel,
        out_shape=pltpu.VMEM((64, 1536), BF16),
        in_specs=[whole()] * 5 + [whole(pltpu.HBM)] * 4,
        out_specs=whole(),
        scratch_shapes=[
            pltpu.VMEM((8, 6, 32, 192), BF16),
            pltpu.VMEM((6, 4, 32, 384), BF16),
            pltpu.VMEM((1728, 1152), BF16),
            pltpu.VMEM((3456, 1152), BF16),
            pltpu.VMEM((3, 8, 32, 128), F32),
            pltpu.VMEM((4, 2, 32, 192), BF16),
            pltpu.VMEM((192, 384), BF16),
            pltpu.SemaphoreType.DMA((56,)),
        ],
        compiler_params=pltpu.CompilerParams(vmem_limit_bytes=40 * MIB),
        cost_estimate=pl.CostEstimate(flops=8 * 10**9, bytes_accessed=13 * 10**6, transcendentals=10**6),
        name="convolutions",
    )(*in_vmem(*blocks), *in_hbm(video, w_in.reshape(27, 192, 384), w_out.reshape(27, 384, 384), w_short))


def fold_kernel(*refs):
    place = here()
    count = (len(refs) - 3) // 2
    w_qkv, out, rows = refs[2 * count :]
    core = place[1] % 2
    rows[:, 128:] = jnp.ones((5120, 128), BF16)
    chips = []
    for same, other in zip(refs[:count], refs[count : 2 * count]):
        for n in range(same.shape[0] // 480):
            s = len(chips)
            chips.append(at_chip(place, s // 4, (0, 1, 3, 2)[s % 4]))
            for ref, at in ((same, core), (other, 1 - core)):
                block = ref[480 * n : 480 * (n + 1)]
                first = pl.multiple_of(640 * s + 320 * at, 32)
                rows[pl.ds(first, 320), :128] = block[:320]
                rows[pl.ds(first, 160), 128:192] = block[320:, :64]
                rows[pl.ds(first + 160, 160), 128:192] = block[320:, 64:]
    total, mean = None, None
    for s, chip in enumerate(chips):
        slab, part = w_qkv[:, pl.ds(pl.multiple_of(chip * 640, 128), 640)], rows[640 * s : 640 * (s + 1)]
        term = jnp.dot(slab, part, preferred_element_type=F32)
        part = jnp.sum(part.astype(F32), axis=0, keepdims=True)
        total = term if total is None else total + term
        mean = part if mean is None else mean + part
    total = total - total[:, 192:193] * (mean * (1.0 / 5120))
    turned = jnp.concatenate([total, jnp.zeros((64, 256), F32)], axis=0).T
    out[...] = turned[:192, :960].astype(BF16)


def fold(same, other, w_qkv):
    return pl.pallas_call(
        fold_kernel,
        out_shape=pltpu.VMEM((192, 960), BF16),
        in_specs=[whole()] * (2 * len(same) + 1),
        out_specs=whole(),
        scratch_shapes=[pltpu.VMEM((5120, 256), BF16)],
        compiler_params=pltpu.CompilerParams(vmem_limit_bytes=20 * MIB),
        cost_estimate=pl.CostEstimate(flops=4 * 10**9, bytes_accessed=12 * 10**6, transcendentals=0),
        name="fold",
    )(*in_vmem(*same, *other, w_qkv.T))


def moments_kernel(layout, *refs):
    place = here()
    count = len(layout)
    pieces, w_embed, out, tokens = (refs[:count], refs[count], refs[count + 1], refs[count + 2])
    for ref, parts in zip(pieces, layout):
        for source, size, block, at in parts:
            tokens[at_rows(place, *block), at : at + size] = ref[source : source + size]
    for g in range(4):
        e = lax.dot_general(
            w_embed[...],
            tokens[4 * g : 4 * g + 4].reshape(256, 1536),
            (((1,), (1,)), ((), ())),
            preferred_element_type=F32,
        )
        mean = jnp.mean(e, axis=0, keepdims=True)
        out[g : g + 1, :] = mean
        out[4 + g : 5 + g, :] = jnp.sum((e - mean) * (e - mean), axis=0, keepdims=True)


def moments(pieces, layout, w_embed):
    return pl.pallas_call(
        lambda *refs: moments_kernel(layout, *refs),
        out_shape=[pltpu.VMEM((8, 256), F32), pltpu.VMEM((16, 64, 1536), BF16)],
        in_specs=[whole()] * (len(pieces) + 1),
        out_specs=[whole(), whole()],
        compiler_params=pltpu.CompilerParams(vmem_limit_bytes=20 * MIB),
        cost_estimate=pl.CostEstimate(flops=2 * 10**9, bytes_accessed=5 * 10**6, transcendentals=0),
        name="moments",
    )(*in_vmem(*pieces), w_embed.T)


def merge_kernel(features, *refs):
    parts, out = [ref[...] for ref in refs[:-1]], refs[-1]
    mean = sum(part[:4] for part in parts) * (1.0 / len(parts))
    spread = sum(part[4:] for part in parts)
    spread = spread + features * sum((part[:4] - mean) * (part[:4] - mean) for part in parts)
    out[:4] = mean
    out[4:] = spread


def merged(parts, features):
    return pl.pallas_call(
        lambda *refs: merge_kernel(features, *refs),
        out_shape=pltpu.VMEM((8, 256), F32),
        in_specs=[whole()] * len(parts),
        out_specs=whole(),
        compiler_params=pltpu.CompilerParams(vmem_limit_bytes=2 * MIB),
        cost_estimate=pl.CostEstimate(flops=10**6, bytes_accessed=10**5, transcendentals=0),
        name="merge",
    )(*in_vmem(*parts))


def most_kernel(layout, tokens, *refs):
    place = here()
    count = len(layout)
    weights, out, folded = (refs[:count], refs[count], refs[count + 1])
    for ref, parts in zip(weights, layout):
        for source, size, block, at in parts:
            folded[pl.ds(pl.multiple_of(at_frames(place, *block) * 192 + at, 96), size), :] = ref[source : source + size]
    folded[pl.ds(pl.multiple_of(at_frames(place, 1, 2) * 192, 192), 192), :] = jnp.zeros((192, 960), BF16)
    for g in range(4):
        x = tokens[4 * g : 4 * g + 4].reshape(256, 1536)
        out[256 * g : 256 * (g + 1)] = jnp.dot(x, folded[...], preferred_element_type=F32)


def project_most(tokens, weights, layout):
    return pl.pallas_call(
        lambda *refs: most_kernel(layout, *refs),
        out_shape=pltpu.VMEM((1024, 960), F32),
        in_specs=[whole()] * (len(weights) + 1),
        out_specs=whole(),
        scratch_shapes=[pltpu.VMEM((1536, 960), BF16)],
        compiler_params=pltpu.CompilerParams(vmem_limit_bytes=20 * MIB),
        cost_estimate=pl.CostEstimate(flops=4 * 10**9, bytes_accessed=8 * 10**6, transcendentals=0),
        name="project_most",
    )(*in_vmem(tokens, *weights))


def last_kernel(tokens, total, low, high, stats, out, folded, staged, sems):
    place = here()
    last = at_frames(place, 1, 2)
    pair, half = last // 2, last % 2
    folded[...] = jnp.zeros((384, 960), BF16)
    folded[pl.ds(pl.multiple_of(half * 192, 192), 96), :] = low[...]
    folded[pl.ds(pl.multiple_of(half * 192 + 96, 96), 96), :] = high[...]
    copies = []
    for g in range(4):
        x = tokens[4 * g : 4 * g + 4, :, pl.ds(pl.multiple_of(pair * 384, 128), 384)].reshape(256, 384)
        acc = total[256 * g : 256 * (g + 1)] + jnp.dot(x, folded[...], preferred_element_type=F32)
        scale = lax.rsqrt(stats[4 + g : 5 + g, :] * (1.0 / 5120) + 1e-06)
        scale = jnp.broadcast_to(scale, (128, 256)).T[:, :1]
        result = (acc * scale).astype(BF16).reshape(4, 4, 16, 960)
        for r in range(4):
            staged[:, 4 * g + r] = result[r]
        copies.append(
            pltpu.make_async_copy(staged.at[:, pl.ds(4 * g, 4)], out.at[:, pl.ds(4 * g, 4)], sems.at[g])
        )
        copies[g].start()
    for copy in copies:
        copy.wait()


def project_last(tokens, total, low, high, stats):
    return pl.pallas_call(
        last_kernel,
        out_shape=jax.ShapeDtypeStruct((4, 16, 16, 960), BF16),
        in_specs=[whole()] * 5,
        out_specs=whole(pltpu.HBM),
        scratch_shapes=[
            pltpu.VMEM((384, 960), BF16),
            pltpu.VMEM((4, 16, 16, 960), BF16),
            pltpu.SemaphoreType.DMA((4,)),
        ],
        compiler_params=pltpu.CompilerParams(vmem_limit_bytes=32 * MIB),
        cost_estimate=pl.CostEstimate(flops=2 * 10**9, bytes_accessed=8 * 10**6, transcendentals=0),
        name="project_last",
    )(*in_vmem(tokens, total, low, high, stats))


def slice_kernel(w_embed, out, slab, sem):
    place = here()
    load = pltpu.make_async_copy(w_embed.at[:, pl.ds(pl.multiple_of(place[0] // 2 * 384, 128), 384)], slab, sem)
    load.start()
    load.wait()
    mine = jnp.where(place[0] % 2 == 0, slab[:, :192], slab[:, 192:])
    out[:320] = mine[:, :128]
    out[320:] = jnp.concatenate([mine[:160, 128:], mine[160:, 128:]], axis=1)


def spliced(name, *targets):
    arrays = []
    for array in [part[0] for target in targets for part in target]:
        if not any(array is other for other in arrays):
            arrays.append(array)
    places = [[next(n for n, a in enumerate(arrays) if a is part[0]) for part in target] for target in targets]

    def kernel(*refs):
        for out, target, sources in zip(refs[len(arrays) :], targets, places):
            at = 0
            for (_, start, size), n in zip(target, sources):
                out[at : at + size] = refs[n][start : start + size]
                at += size

    rows = [sum(part[2] for part in target) for target in targets]
    columns = targets[0][0][0].shape[1]
    return pl.pallas_call(
        kernel,
        out_shape=[pltpu.VMEM((n, columns), BF16) for n in rows],
        in_specs=[whole()] * len(arrays),
        out_specs=[whole()] * len(targets),
        compiler_params=pltpu.CompilerParams(vmem_limit_bytes=8 * MIB),
        cost_estimate=pl.CostEstimate(flops=10**6, bytes_accessed=10**6, transcendentals=0),
        name=name,
    )(*in_vmem(*arrays))


def embed_slice(w_embed):
    return pl.pallas_call(
        slice_kernel,
        out_shape=pltpu.VMEM((480, 128), BF16),
        in_specs=[whole(pltpu.HBM)],
        out_specs=whole(),
        scratch_shapes=[pltpu.VMEM((320, 384), BF16), pltpu.SemaphoreType.DMA],
        cost_estimate=pl.CostEstimate(flops=10**6, bytes_accessed=10**6, transcendentals=0),
        name="embed_slice",
    )(*in_hbm(w_embed.T))


def shards(video, w_conv_in, w_conv_out, w_shortcut, w_embed, w_qkv):
    back = by_frames(video, NEXT_FRAMES)
    back_chip = lax.ppermute(video, ("frames", "rows"), NEXT_FRAMES_SWAP_CHIP)
    side_core, side_chip = by_rows(video, SWAP_CORE), by_rows(video, SWAP_CHIP)
    mine = embed_slice(w_embed)
    along = [by_rows(mine, swap_z(k)) for k in (1, 3, 2)]
    along, back, back_chip, side_chip = lax.optimization_barrier((along, back, back_chip, side_chip))
    back_core = by_rows(back, SWAP_CORE)
    (four,) = spliced("embed_four", [(mine, 0, 480)] + [(part, 0, 480) for part in along])
    patches = convolutions(
        video, (side_core, side_chip, back, back_core, back_chip), w_conv_in, w_conv_out, w_shortcut
    )
    across = by_rows(four, SWAP_Y_LO)
    across, patches = lax.optimization_barrier((across, patches))
    folded = fold([four, across], [by_rows(four, SWAP_CORE), by_rows(across, SWAP_CORE)], w_qkv)

    opposite = by_rows(patches, SWAP_Y_LO)
    opposite, folded = lax.optimization_barrier((opposite, folded))
    (pair,) = spliced("patch_pair", [(patches, 0, 64), (opposite, 0, 64)])
    from_low, from_high = by_rows(pair, swap_z(1)), by_rows(pair, swap_z(3))
    from_left, from_right = by_frames(folded, swap_x(1)), by_frames(folded, swap_x(3))
    across = by_frames(folded, SWAP_Y_HI)
    from_low, from_high, from_left, from_right, across = lax.optimization_barrier(
        (from_low, from_high, from_left, from_right, across)
    )
    up, down = spliced("patch_ends", [(from_low, 0, 64)], [(from_high, 64, 64)])
    last_low, last_high = by_rows(up, swap_z(3)), by_rows(down, swap_z(1))
    (most,) = spliced("patch_most", [(pair, 0, 128), (from_low, 0, 128), (from_high, 0, 128)])
    groups = [most, last_low, last_high]
    pieces = groups + [by_rows(group, SWAP_CORE) for group in groups]
    pieces_layout = [
        layout
        for core in (0, 1)
        for layout in (
            [(64 * n, 64, (n % 2, (0, 1, 3)[n // 2], core), 0) for n in range(6)],
            [(0, 64, (0, 2, core), 0)],
            [(0, 64, (1, 2, core), 0)],
        )
    ]

    to_right, to_left = spliced(
        "fold_parts", ((from_left, 0, 96), (across, 0, 192)), ((from_right, 96, 96), (across, 0, 192))
    )
    far_left, far_right = by_frames(to_right, swap_x(3)), by_frames(to_left, swap_x(1))
    to_right, to_left = spliced("fold_ends", ((far_left, 96, 96),), ((far_right, 192, 96),))
    last_left, last_right = by_frames(to_right, swap_x(1)), by_frames(to_left, swap_x(3))
    weights = [folded, from_left, from_right, across, far_left, far_right]
    weights_layout = [
        [(0, 192, (0, 0), 0)],
        [(0, 192, (0, 1), 0)],
        [(0, 192, (0, 3), 0)],
        [(0, 192, (1, 0), 0)],
        [(0, 96, (0, 2), 0), (96, 192, (1, 3), 0)],
        [(0, 96, (0, 2), 96), (96, 192, (1, 1), 0)],
    ]

    stats, tokens = moments(pieces, pieces_layout, w_embed)
    total = project_most(tokens, weights, weights_layout)
    for pairs, features in ((SWAP_Y_LO, 320), (swap_z(1), 640), (swap_z(3), 1280), (SWAP_CORE, 2560)):
        swapped = by_rows(stats, pairs)
        if features == 1280:
            swapped, total = lax.optimization_barrier((swapped, total))
        stats = merged([stats, swapped], features)
    return project_last(tokens, total, last_left, last_right, stats)


def solution(mesh):
    placed = (P("frames", "rows", None, None), P(), P(), P(), P(None, "rows"), P(None, "rows"))
    return jax.shard_map(
        shards,
        mesh=mesh,
        in_specs=placed,
        out_specs=P("frames", None, None, "rows"),
        check_vma=False,
    )
```
